128 devices in a mesh: seq: 16 (over y_lo, x, core), ch: 8 (over z, y_hi).
Axes of the slice: x: 4, y: 4 (y_hi: 2, y_lo: 2; y = y_hi * 2 + y_lo), z: 4, core: 2. Of those that a mesh axis runs over, the one named last changes fastest.
Arguments:
- gate_input: bfloat16 [2048, 8192], P('seq', 'ch'), may hold values from -6 to 6
- value_input: bfloat16 [2048, 8192], P('seq', 'ch'), may hold values from -6 to 6
- filter_taps: float32 [2048, 8192], P('seq', 'ch'), may hold values from -1.5 to 1.5
- out_weight: bfloat16 [8192, 8192], P('ch'), may hold values from -0.0625 to 0.0625
- grad_output: bfloat16 [2048, 8192], P('seq', 'ch'), may hold values from -6 to 6
Outputs:
- block_output: bfloat16 [2048, 8192], P('seq', 'ch')
- gate_grad: bfloat16 [2048, 8192], P('seq', 'ch')
- value_grad: bfloat16 [2048, 8192], P('seq', 'ch')
- filter_grad: float32 [2048, 8192], P('seq', 'ch')
- weight_grad: bfloat16 [8192, 8192], P('ch', 'seq')
The draws below stay inside these ranges and needn't reach their ends.
All inputs are finite; a program needn't handle non-finite values.
Results may differ from the reference program's by a relative error of at most 0.017.
Values may be sent and summed in bfloat16 or wider, within the bound.
No kernel may reach another device: no remote copies, remote signals or barrier semaphores. Data moves between devices by JAX's collectives and lax.ppermute only.
A program may use at most 128 MiB of HBM per device.

```python
import math
import jax
import jax.numpy as jnp

D = 8192
LENGTH = 2048


def draw_filter_taps(key, part):
    key = jax.random.fold_in(key, 11)
    span_key, jitter_key = jax.random.split(key)
    lowest = math.log(16.0)
    highest = math.log(LENGTH * 4.0)
    decay_span = jnp.exp(jax.random.uniform(span_key, (1, D), jnp.float32, lowest, highest))
    jitter = jnp.clip(jax.random.normal(jitter_key, (LENGTH, D), jnp.float32), -4.0, 4.0)
    offsets = jnp.arange(LENGTH, dtype=jnp.float32)[:, None]
    amplitude = jnp.sqrt(1.0 / jnp.minimum(decay_span * 0.5, LENGTH * 1.0))
    return jitter * amplitude * jnp.exp(-offsets / decay_span)


def block_levels(key, dims, shards, least, largest):
    loudness, own = 1.0, jax.random.fold_in(key, 6)
    for position, shards_of in shards:
        steps = jnp.exp(jax.random.uniform(jax.random.fold_in(own, position), (shards_of,), jnp.float32, least / len(shards), largest / len(shards)))
        loudness = loudness * jnp.repeat(steps, dims[position] // shards_of).reshape([-1 if axis == position else 1 for axis in range(len(dims))])
    return loudness


def normal_values(own_key, dims, width, most, shards=(), kind=jnp.bfloat16):
    array = jax.random.normal(own_key, dims, jnp.float32) * width
    if len(shards) > 0:
        array = block_levels(own_key, dims, shards, -0.22, 0.18) * array
    return jnp.clip(array, min=-most, max=most).astype(kind)


def setup_inputs(seed: int = 0) -> dict:
    arg_keys = jax.random.split(jax.random.key(seed), 6)
    gate_input = normal_values(arg_keys[0], (LENGTH, D), 1.0, 6.0, ((0, 16), (1, 8)))
    value_input = normal_values(arg_keys[1], (LENGTH, D), 1.0, 6.0, ((0, 16), (1, 8)))
    filter_taps = draw_filter_taps(jax.random.fold_in(arg_keys[5], 71), 0)
    out_weight = normal_values(arg_keys[3], (D, D), D ** -0.5, 0.0625, ((0, 8),))
    grad_output = normal_values(arg_keys[4], (LENGTH, D), 1.0, 6.0, ((0, 16), (1, 8)))
    return dict(gate_input=gate_input, value_input=value_input, filter_taps=filter_taps, out_weight=out_weight, grad_output=grad_output)


def causal_product(former, latter, conjugate):
    length_here = former.shape[0]
    spec_former = jnp.fft.rfft(former, n=2 * length_here, axis=0)
    spec_latter = jnp.fft.rfft(latter, n=2 * length_here, axis=0)
    if conjugate:
        spec_former = jnp.conj(spec_former)
    return jnp.fft.irfft(spec_former * spec_latter, n=2 * length_here, axis=0)[:length_here]

def reference(gate_input, value_input, filter_taps, out_weight, grad_output):
    gate_wide = gate_input.astype(jnp.float32)
    value_wide = value_input.astype(jnp.float32)
    convolved = causal_product(filter_taps, value_wide, False).astype(jnp.float32)
    gated = (gate_wide * convolved).astype(jnp.bfloat16)
    block_output = jnp.dot(gated, out_weight, preferred_element_type=jnp.float32).astype(jnp.bfloat16)
    pre_grad = jnp.dot(grad_output, out_weight.T, preferred_element_type=jnp.float32)
    gate_grad = (pre_grad * convolved).astype(jnp.bfloat16)
    conv_grad = pre_grad * gate_wide
    value_grad = causal_product(filter_taps, conv_grad, True).astype(jnp.bfloat16)
    grad_scale = 1.0 / math.sqrt(LENGTH)
    filter_grad = (causal_product(value_wide, conv_grad, True) * grad_scale).astype(jnp.float32)
    weight_grad = (jnp.dot(gated.T, grad_output, preferred_element_type=jnp.float32) * grad_scale).astype(jnp.bfloat16)
    return (block_output, gate_grad, value_grad, filter_grad, weight_grad)
```

```python
import functools
import math

import jax
import jax.numpy as jnp
import numpy as np
from jax import lax
from jax.experimental import pallas as pl
from jax.experimental.pallas import tpu as pltpu
from jax.sharding import PartitionSpec as P

BLOCKS = 16
INNER = 128
PERIOD = 2 * BLOCKS * INNER
HALF = 64
GROUP = 16
BF16 = jnp.bfloat16
F32 = jnp.float32


def plane_order():
    order = [(0, False), (BLOCKS, False)]
    for freq in range(1, BLOCKS):
        order += [(freq, False), (freq, True)]
    return order


def outer_matrices():
    blocks = np.arange(BLOCKS)
    forward = np.zeros((2 * BLOCKS, BLOCKS))
    inverse = np.zeros((BLOCKS, 2 * BLOCKS))
    for plane, (freq, imaginary) in enumerate(plane_order()):
        turn = 2.0 * np.pi * ((freq * blocks) % (2 * BLOCKS)) / (2 * BLOCKS)
        weight = (1.0 if freq in (0, BLOCKS) else 2.0) / PERIOD
        wave = -np.sin(turn) if imaginary else np.cos(turn)
        forward[plane] = wave
        inverse[:, plane] = weight * wave
    eye = np.eye(GROUP)
    return np.kron(forward, eye), np.kron(inverse, eye)


def inner_matrices():
    freqs = np.arange(BLOCKS + 1)[:, None, None] + 2 * BLOCKS * np.arange(INNER)[None, :, None]
    turn = 2.0 * np.pi * ((freqs * np.arange(INNER)[None, None, :]) % PERIOD) / PERIOD
    cos, sin = np.cos(turn), np.sin(turn)
    top = np.concatenate([cos, sin], axis=2)
    bottom = np.concatenate([-sin, cos], axis=2)
    forward = np.concatenate([top, bottom], axis=1)
    return forward, np.swapaxes(forward, 1, 2)


def dot(left, right):
    return jnp.dot(left, right, preferred_element_type=F32)


def lane_low(shape):
    return lax.broadcasted_iota(jnp.int32, shape, len(shape) - 1) < HALF


def swap(array):
    return pltpu.roll(array, HALF, array.ndim - 1)


def pack_kernel(value_ref, taps_ref, out_ref):
    for pair in range(value_ref.shape[1] // INNER):
        lanes = pl.ds(pair * INNER, INNER)
        value = value_ref[:, lanes].astype(F32)
        taps = taps_ref[:, lanes]
        low = lane_low(value.shape)
        out_ref[2 * pair] = jnp.where(low, value, swap(taps)).astype(BF16)
        out_ref[2 * pair + 1] = jnp.where(low, swap(value), taps).astype(BF16)


def outer_forward(read_group, outer_ref, planes_ref):
    for group in range(INNER // GROUP):
        rows = pl.ds(group * GROUP, GROUP)
        block = read_group(rows).reshape(BLOCKS * GROUP, INNER)
        wide = dot(outer_ref[...], block).astype(BF16)
        planes_ref[:, rows, :] = wide.reshape(2 * BLOCKS, GROUP, INNER)


def inner_forward(freq, inner_ref, planes_ref):
    if freq in (0, BLOCKS):
        return dot(inner_ref[freq, :, :INNER], planes_ref[0 if freq == 0 else 1])
    pair = planes_ref[2 * freq : 2 * freq + 2].reshape(2 * INNER, INNER)
    return dot(inner_ref[freq], pair)


def inner_inverse(freq, product, inner_ref, planes_ref):
    if freq in (0, BLOCKS):
        planes_ref[0 if freq == 0 else 1] = dot(inner_ref[freq, :INNER, :], product).astype(BF16)
    else:
        back = dot(inner_ref[freq], product).astype(BF16)
        planes_ref[2 * freq : 2 * freq + 2] = back.reshape(2, INNER, INNER)


def outer_inverse(group, outer_ref, planes_ref):
    planes = planes_ref[:, pl.ds(group * GROUP, GROUP), :].reshape(2 * BLOCKS * GROUP, INNER)
    return dot(outer_ref[...], planes).reshape(BLOCKS, GROUP, INNER)


def convolve_kernel(pair_ref, outer_ref, inner_ref, inner_back_ref, outer_back_ref, out_ref, spec_ref, planes_ref, back_ref):
    outer_forward(lambda rows: pair_ref[:, rows, :], outer_ref, planes_ref)
    for freq in range(BLOCKS + 1):
        spec = inner_forward(freq, inner_ref, planes_ref)
        spec_ref[freq] = spec.astype(BF16)
        other = swap(spec)
        re, im = spec[:INNER], spec[INNER:]
        other_re, other_im = other[:INNER], other[INNER:]
        product = jnp.concatenate([re * other_re - im * other_im, re * other_im + im * other_re], 0)
        inner_inverse(freq, product.astype(BF16), inner_back_ref, back_ref)
    half_groups = INNER // GROUP // 2
    for group in range(half_groups):
        first = outer_inverse(group, outer_back_ref, back_ref)
        second = outer_inverse(group + half_groups, outer_back_ref, back_ref)
        packed = jnp.where(lane_low(first.shape), first, second)
        out_ref[:, pl.ds(group * GROUP, GROUP), :] = packed.astype(BF16)


def correlate_kernel(grad_ref, spec_ref, outer_ref, inner_ref, inner_back_ref, outer_back_ref, out_ref, wide_ref, planes_ref, back_ref):
    for block in range(BLOCKS):
        packed = grad_ref[block].astype(F32)
        turned = swap(packed)
        low = lane_low(packed.shape)
        wide_ref[block, :HALF] = jnp.where(low, packed, turned).astype(BF16)
        wide_ref[block, HALF:] = jnp.where(low, turned, packed).astype(BF16)
    outer_forward(lambda rows: wide_ref[:, rows, :], outer_ref, planes_ref)
    for freq in range(BLOCKS + 1):
        grad = inner_forward(freq, inner_ref, planes_ref)
        spec = spec_ref[freq].astype(F32)
        re, im = spec[:INNER], spec[INNER:]
        grad_re, grad_im = grad[:INNER], grad[INNER:]
        product = jnp.concatenate([re * grad_re + im * grad_im, re * grad_im - im * grad_re], 0)
        inner_inverse(freq, product.astype(BF16), inner_back_ref, back_ref)
    for group in range(INNER // GROUP):
        out_ref[:, pl.ds(group * GROUP, GROUP), :] = outer_inverse(group, outer_back_ref, back_ref).astype(BF16)


def gate_kernel(recv_ref, gate_ref, conv_ref, gated_ref):
    for pair in range(BLOCKS // 2):
        first = recv_ref[2 * pair].astype(F32)
        second = recv_ref[2 * pair + 1].astype(F32)
        low = lane_low(first.shape)
        conv = jnp.concatenate([jnp.where(low, first, swap(second)), jnp.where(low, swap(first), second)], 0)
        lanes = pl.ds(pair * INNER, INNER)
        conv_ref[:, lanes] = conv
        gated_ref[:, lanes] = (gate_ref[:, lanes].astype(F32) * conv).astype(BF16)


def finish_kernel(scale, recv_ref, value_grad_ref, filter_grad_ref):
    for pair in range(BLOCKS // 2):
        first = recv_ref[2 * pair].astype(F32)
        second = recv_ref[2 * pair + 1].astype(F32)
        low = lane_low(first.shape)
        lanes = pl.ds(pair * INNER, INNER)
        filter_grad_ref[:, lanes] = jnp.where(low, first, swap(second)) * scale
        value_grad_ref[:, lanes] = jnp.where(low, swap(first), second).astype(BF16)


def pre_grad_kernel(grad_ref, weight_ref, gate_ref, pre_ref, cotangent_ref, columns_ref):
    step = pl.program_id(0)
    grad = grad_ref[0]
    part = lax.dot_general(grad, weight_ref[...], (((1,), (1,)), ((), ())), preferred_element_type=F32)
    width = columns_ref.shape[2]
    for piece in range(columns_ref.shape[0]):
        columns_ref[piece] = grad[:, piece * width : (piece + 1) * width]

    @pl.when(step == 0)
    def _():
        pre_ref[...] = part

    @pl.when(step > 0)
    def _():
        pre_ref[...] += part

    @pl.when(step == pl.num_programs(0) - 1)
    def _():
        for pair in range(BLOCKS // 2):
            lanes = pl.ds(pair * INNER, INNER)
            cotangent = pre_ref[:, lanes] * gate_ref[:, lanes].astype(F32)
            top, bottom = cotangent[:HALF], cotangent[HALF:]
            low = lane_low(top.shape)
            cotangent_ref[2 * pair] = jnp.where(low, top, swap(bottom)).astype(BF16)
            cotangent_ref[2 * pair + 1] = jnp.where(low, swap(top), bottom).astype(BF16)


def project_kernel(gated_ref, weight_ref, out_ref):
    out_ref[0] = dot(gated_ref[...], weight_ref[...]).astype(BF16)


def shape(dims, kind):
    return jax.ShapeDtypeStruct(dims, kind)


def params(mebibytes=48):
    return pltpu.CompilerParams(vmem_limit_bytes=mebibytes * 1024 * 1024)


def exchange(array, axis):
    return lax.all_to_all(array, axis, split_axis=0, concat_axis=0, tiled=True)


def body(gate_input, value_input, filter_taps, out_weight, grad_output):
    rows, channels = gate_input.shape
    shards = lax.axis_size("seq")
    groups = lax.axis_size("ch")
    scale = 1.0 / math.sqrt(rows * shards)
    width = channels * groups // shards
    outer, outer_back = (jnp.asarray(m, BF16) for m in outer_matrices())
    inner, inner_back = (jnp.asarray(m, BF16) for m in inner_matrices())
    planes = pltpu.VMEM((2 * BLOCKS, INNER, INNER), BF16)

    pair = pl.pallas_call(
        pack_kernel, out_shape=shape((shards, rows, INNER), BF16), compiler_params=params(), name="pack_pair"
    )(value_input, filter_taps)
    pair = exchange(pair, "seq")
    grad_full = exchange(jnp.broadcast_to(grad_output[None], (groups, rows, channels)), "ch")

    packed, spec = pl.pallas_call(
        convolve_kernel,
        out_shape=(shape((shards, HALF, INNER), BF16), shape((BLOCKS + 1, 2 * INNER, INNER), BF16)),
        scratch_shapes=[planes, planes],
        compiler_params=params(),
        name="convolve",
    )(pair, outer, inner, inner_back, outer_back)
    conv, gated = pl.pallas_call(
        gate_kernel,
        out_shape=(shape((rows, channels), F32), shape((rows, channels), BF16)),
        compiler_params=params(),
        name="gate",
    )(exchange(packed, "seq"), gate_input)
    gated_all = lax.all_gather(gated, "seq", axis=0, tiled=True)

    whole = lambda *dims: pl.BlockSpec(dims, lambda step: (0,) * len(dims))
    pre_grad, cotangent, columns = pl.pallas_call(
        pre_grad_kernel,
        grid=(groups,),
        in_specs=[
            pl.BlockSpec((1, rows, channels), lambda step: (step, 0, 0)),
            pl.BlockSpec((channels, channels), lambda step: (0, step)),
            whole(rows, channels),
        ],
        out_specs=(
            whole(rows, channels),
            whole(shards, HALF, INNER),
            pl.BlockSpec((shards // groups, rows, width), lambda step: (step, 0, 0)),
        ),
        out_shape=(
            shape((rows, channels), F32),
            shape((shards, HALF, INNER), BF16),
            shape((shards, rows, width), BF16),
        ),
        compiler_params=params(),
        name="pre_grad",
    )(grad_full, out_weight, gate_input)
    gate_grad = (pre_grad * conv).astype(BF16)

    returned = pl.pallas_call(
        correlate_kernel,
        out_shape=shape((shards, rows, INNER), BF16),
        scratch_shapes=[pltpu.VMEM((BLOCKS, INNER, INNER), BF16), planes, planes],
        compiler_params=params(),
        name="correlate",
    )(exchange(cotangent, "seq"), spec, outer, inner, inner_back, outer_back)
    value_grad, filter_grad = pl.pallas_call(
        functools.partial(finish_kernel, scale),
        out_shape=(shape((rows, channels), BF16), shape((rows, channels), F32)),
        compiler_params=params(),
        name="finish",
    )(exchange(returned, "seq"))

    projected = pl.pallas_call(
        project_kernel,
        grid=(groups,),
        in_specs=[whole(rows, channels), pl.BlockSpec((channels, channels), lambda step: (0, step))],
        out_specs=pl.BlockSpec((1, rows, channels), lambda step: (step, 0, 0)),
        out_shape=shape((groups, rows, channels), BF16),
        compiler_params=params(),
        name="project",
    )(gated, out_weight)
    block_output = jnp.sum(exchange(projected, "ch").astype(F32), axis=0).astype(BF16)

    columns = exchange(columns, "seq").reshape(shards * rows, width)
    summed = lax.dot_general(gated_all, columns, (((0,), (0,)), ((), ())), preferred_element_type=F32)
    weight_grad = (summed * scale).astype(BF16)
    return (block_output, gate_grad, value_grad, filter_grad, weight_grad)


def solution(mesh):
    placed = (P("seq", "ch"), P("seq", "ch"), P("seq", "ch"), P("ch", None), P("seq", "ch"))
    return jax.shard_map(
        body,
        mesh=mesh,
        in_specs=placed,
        out_specs=(P("seq", "ch"), P("seq", "ch"), P("seq", "ch"), P("seq", "ch"), P("ch", "seq")),
        check_vma=False,
    )
```

```python
import functools
import math

import jax
import jax.numpy as jnp
import numpy as np
from jax import lax
from jax.experimental import pallas as pl
from jax.experimental.pallas import tpu as pltpu
from jax.sharding import PartitionSpec as P

BLOCKS = 16
INNER = 128
PERIOD = 2 * BLOCKS * INNER
HALF = 64
GROUP = 16
BF16 = jnp.bfloat16
F32 = jnp.float32


def plane_order():
    order = [(0, False), (BLOCKS, False)]
    for freq in range(1, BLOCKS):
        order += [(freq, False), (freq, True)]
    return order


def outer_matrices():
    blocks = np.arange(BLOCKS)
    forward = np.zeros((2 * BLOCKS, BLOCKS))
    inverse = np.zeros((BLOCKS, 2 * BLOCKS))
    for plane, (freq, imaginary) in enumerate(plane_order()):
        turn = 2.0 * np.pi * ((freq * blocks) % (2 * BLOCKS)) / (2 * BLOCKS)
        weight = (1.0 if freq in (0, BLOCKS) else 2.0) / PERIOD
        wave = -np.sin(turn) if imaginary else np.cos(turn)
        forward[plane] = wave
        inverse[:, plane] = weight * wave
    eye = np.eye(GROUP)
    return np.kron(forward, eye), np.kron(inverse, eye)


def inner_matrices():
    freqs = np.arange(BLOCKS + 1)[:, None, None] + 2 * BLOCKS * np.arange(INNER)[None, :, None]
    turn = 2.0 * np.pi * ((freqs * np.arange(INNER)[None, None, :]) % PERIOD) / PERIOD
    cos, sin = np.cos(turn), np.sin(turn)
    top = np.concatenate([cos, sin], axis=2)
    bottom = np.concatenate([-sin, cos], axis=2)
    forward = np.concatenate([top, bottom], axis=1)
    return forward, np.swapaxes(forward, 1, 2)


def dot(left, right):
    return jnp.dot(left, right, preferred_element_type=F32)


def lane_low(shape):
    return lax.broadcasted_iota(jnp.int32, shape, len(shape) - 1) < HALF


def swap(array):
    return pltpu.roll(array, HALF, array.ndim - 1)


def pack_kernel(value_ref, taps_ref, out_ref):
    for pair in range(value_ref.shape[1] // INNER):
        lanes = pl.ds(pair * INNER, INNER)
        value = value_ref[:, lanes].astype(F32)
        taps = taps_ref[:, lanes]
        low = lane_low(value.shape)
        out_ref[2 * pair] = jnp.where(low, value, swap(taps)).astype(BF16)
        out_ref[2 * pair + 1] = jnp.where(low, swap(value), taps).astype(BF16)


def outer_forward(read_group, outer_ref, planes_ref):
    for group in range(INNER // GROUP):
        rows = pl.ds(group * GROUP, GROUP)
        block = read_group(rows).reshape(BLOCKS * GROUP, INNER)
        wide = dot(outer_ref[...], block).astype(BF16)
        planes_ref[:, rows, :] = wide.reshape(2 * BLOCKS, GROUP, INNER)


def inner_forward(freq, inner_ref, planes_ref):
    if freq in (0, BLOCKS):
        return dot(inner_ref[freq, :, :INNER], planes_ref[0 if freq == 0 else 1])
    pair = planes_ref[2 * freq : 2 * freq + 2].reshape(2 * INNER, INNER)
    return dot(inner_ref[freq], pair)


def inner_inverse(freq, product, inner_ref, planes_ref):
    if freq in (0, BLOCKS):
        planes_ref[0 if freq == 0 else 1] = dot(inner_ref[freq, :INNER, :], product).astype(BF16)
    else:
        back = dot(inner_ref[freq], product).astype(BF16)
        planes_ref[2 * freq : 2 * freq + 2] = back.reshape(2, INNER, INNER)


def outer_inverse(group, outer_ref, planes_ref):
    planes = planes_ref[:, pl.ds(group * GROUP, GROUP), :].reshape(2 * BLOCKS * GROUP, INNER)
    return dot(outer_ref[...], planes).reshape(BLOCKS, GROUP, INNER)


def convolve_kernel(pair_ref, outer_ref, inner_ref, inner_back_ref, outer_back_ref, out_ref, spec_ref, planes_ref, back_ref):
    outer_forward(lambda rows: pair_ref[:, rows, :], outer_ref, planes_ref)
    for freq in range(BLOCKS + 1):
        spec = inner_forward(freq, inner_ref, planes_ref)
        spec_ref[freq] = spec.astype(BF16)
        other = swap(spec)
        re, im = spec[:INNER], spec[INNER:]
        other_re, other_im = other[:INNER], other[INNER:]
        product = jnp.concatenate([re * other_re - im * other_im, re * other_im + im * other_re], 0)
        inner_inverse(freq, product.astype(BF16), inner_back_ref, back_ref)
    half_groups = INNER // GROUP // 2
    for group in range(half_groups):
        first = outer_inverse(group, outer_back_ref, back_ref)
        second = outer_inverse(group + half_groups, outer_back_ref, back_ref)
        packed = jnp.where(lane_low(first.shape), first, second)
        out_ref[:, pl.ds(group * GROUP, GROUP), :] = packed.astype(BF16)


def correlate_kernel(grad_ref, spec_ref, outer_ref, inner_ref, inner_back_ref, outer_back_ref, out_ref, wide_ref, planes_ref, back_ref):
    for block in range(BLOCKS):
        packed = grad_ref[block].astype(F32)
        turned = swap(packed)
        low = lane_low(packed.shape)
        wide_ref[block, :HALF] = jnp.where(low, packed, turned).astype(BF16)
        wide_ref[block, HALF:] = jnp.where(low, turned, packed).astype(BF16)
    outer_forward(lambda rows: wide_ref[:, rows, :], outer_ref, planes_ref)
    for freq in range(BLOCKS + 1):
        grad = inner_forward(freq, inner_ref, planes_ref)
        spec = spec_ref[freq].astype(F32)
        re, im = spec[:INNER], spec[INNER:]
        grad_re, grad_im = grad[:INNER], grad[INNER:]
        product = jnp.concatenate([re * grad_re + im * grad_im, re * grad_im - im * grad_re], 0)
        inner_inverse(freq, product.astype(BF16), inner_back_ref, back_ref)
    for group in range(INNER // GROUP):
        out_ref[:, pl.ds(group * GROUP, GROUP), :] = outer_inverse(group, outer_back_ref, back_ref).astype(BF16)


def gate_kernel(recv_ref, gate_ref, conv_ref, gated_ref):
    for pair in range(BLOCKS // 2):
        first = recv_ref[2 * pair].astype(F32)
        second = recv_ref[2 * pair + 1].astype(F32)
        low = lane_low(first.shape)
        conv = jnp.concatenate([jnp.where(low, first, swap(second)), jnp.where(low, swap(first), second)], 0)
        lanes = pl.ds(pair * INNER, INNER)
        conv_ref[:, lanes] = conv
        gated_ref[:, lanes] = (gate_ref[:, lanes].astype(F32) * conv).astype(BF16)


def finish_kernel(scale, recv_ref, value_grad_ref, filter_grad_ref):
    for pair in range(BLOCKS // 2):
        first = recv_ref[2 * pair].astype(F32)
        second = recv_ref[2 * pair + 1].astype(F32)
        low = lane_low(first.shape)
        lanes = pl.ds(pair * INNER, INNER)
        filter_grad_ref[:, lanes] = jnp.where(low, first, swap(second)) * scale
        value_grad_ref[:, lanes] = jnp.where(low, swap(first), second).astype(BF16)


def pre_grad_kernel(grad_ref, weight_ref, gate_ref, conv_ref, gate_grad_ref, cotangent_ref, total_ref):
    step = pl.program_id(0)
    width = grad_ref.shape[2]
    part = 0.0
    for piece in range(grad_ref.shape[0]):
        weight = weight_ref[:, piece * width : (piece + 1) * width]
        part += lax.dot_general(weight, grad_ref[piece], (((1,), (1,)), ((), ())), preferred_element_type=F32)

    @pl.when(step == 0)
    def _():
        total_ref[...] = part

    @pl.when(step > 0)
    def _():
        total_ref[...] += part

    @pl.when(step == pl.num_programs(0) - 1)
    def _():
        for pair in range(BLOCKS // 2):
            lanes = pl.ds(pair * INNER, INNER)
            pre = total_ref[lanes, :].T
            gate_grad_ref[:, lanes] = (pre * conv_ref[:, lanes]).astype(BF16)
            cotangent = pre * gate_ref[:, lanes].astype(F32)
            top, bottom = cotangent[:HALF], cotangent[HALF:]
            low = lane_low(top.shape)
            cotangent_ref[2 * pair] = jnp.where(low, top, swap(bottom)).astype(BF16)
            cotangent_ref[2 * pair + 1] = jnp.where(low, swap(top), bottom).astype(BF16)


def project_kernel(spot_ref, gated_ref, weight_ref, *out_refs):
    step = pl.program_id(0)
    block = dot(gated_ref[...], weight_ref[...]).astype(BF16)
    for turn, out_ref in enumerate(out_refs):

        @pl.when(step // 2 == turn)
        def _():
            out_ref[0] = block


def shape(dims, kind):
    return jax.ShapeDtypeStruct(dims, kind)


def params(mebibytes=16):
    return pltpu.CompilerParams(vmem_limit_bytes=mebibytes * 1024 * 1024)


def exchange(array, axis):
    return lax.all_to_all(array, axis, split_axis=0, concat_axis=0, tiled=True)


def body(gate_input, value_input, filter_taps, out_weight, grad_output):
    rows, channels = gate_input.shape
    shards = lax.axis_size("seq")
    groups = lax.axis_size("ch")
    scale = 1.0 / math.sqrt(rows * shards)
    width = channels * groups // shards
    outer, outer_back = (jnp.asarray(m, BF16) for m in outer_matrices())
    inner, inner_back = (jnp.asarray(m, BF16) for m in inner_matrices())
    planes = pltpu.VMEM((2 * BLOCKS, INNER, INNER), BF16)

    pair = pl.pallas_call(
        pack_kernel, out_shape=shape((shards, rows, INNER), BF16), compiler_params=params(), name="pack_pair"
    )(value_input, filter_taps)
    pair = exchange(pair, "seq")
    place = lax.axis_index("ch")
    ring = groups // 2
    spot = jnp.stack([place // 2, place % 2]).astype(jnp.int32)
    halves = jnp.stack([grad_output[:, :width], grad_output[:, width:]])
    across = lax.ppermute(halves, "ch", [(i, i ^ 1) for i in range(groups)])
    even = spot[1] == 0
    sides = jnp.concatenate([jnp.where(even, halves, across), jnp.where(even, across, halves)], 0)
    grad_full = lax.all_gather(
        sides, "ch", axis=0, tiled=True, axis_index_groups=[[2 * i + j for i in range(ring)] for j in range(2)]
    )

    packed, spec = pl.pallas_call(
        convolve_kernel,
        out_shape=(shape((shards, HALF, INNER), BF16), shape((BLOCKS + 1, 2 * INNER, INNER), BF16)),
        scratch_shapes=[planes, planes],
        compiler_params=params(),
        name="convolve",
    )(pair, outer, inner, inner_back, outer_back)
    conv, gated = pl.pallas_call(
        gate_kernel,
        out_shape=(shape((rows, channels), F32), shape((rows, channels), BF16)),
        compiler_params=params(),
        name="gate",
    )(exchange(packed, "seq"), gate_input)
    gated_all = lax.all_gather(gated, "seq", axis=0, tiled=True)

    whole = lambda *dims: pl.BlockSpec(dims, lambda step, spot: (0,) * len(dims))
    columns = exchange(grad_full, "seq")
    fixed = lambda *dims: pl.BlockSpec(dims, lambda step: (0,) * len(dims))
    gate_grad, cotangent = pl.pallas_call(
        pre_grad_kernel,
        grid=(groups,),
        in_specs=[
            pl.BlockSpec((shards // groups, rows, width), lambda step: (step, 0, 0)),
            pl.BlockSpec((channels, channels), lambda step: (0, step)),
            fixed(rows, channels),
            fixed(rows, channels),
        ],
        out_specs=(fixed(rows, channels), fixed(shards, HALF, INNER)),
        out_shape=(shape((rows, channels), BF16), shape((shards, HALF, INNER), BF16)),
        scratch_shapes=[pltpu.VMEM((channels, rows), F32)],
        compiler_params=params(52),
        name="pre_grad",
    )(grad_full, out_weight, gate_input, conv)
    cotangent, columns = lax.optimization_barrier((cotangent, columns))

    returned = pl.pallas_call(
        correlate_kernel,
        out_shape=shape((shards, rows, INNER), BF16),
        scratch_shapes=[pltpu.VMEM((BLOCKS, INNER, INNER), BF16), planes, planes],
        compiler_params=params(),
        name="correlate",
    )(exchange(cotangent, "seq"), spec, outer, inner, inner_back, outer_back)
    value_grad, filter_grad = pl.pallas_call(
        functools.partial(finish_kernel, scale),
        out_shape=(shape((rows, channels), BF16), shape((rows, channels), F32)),
        compiler_params=params(),
        name="finish",
    )(exchange(returned, "seq"))

    order = (2, 1, 3, 0)

    def weight_block(step, spot):
        turn = step // 2
        ahead = jnp.where(turn == 0, 2, jnp.where(turn == 1, 1, jnp.where(turn == 2, 3, 0)))
        return 0, lax.rem(spot[0] + ahead, ring) * 2 + (step ^ spot[1]) % 2

    def out_block(turn):
        return lambda step, spot: (jnp.clip(step - 2 * turn, 0, 1), 0, 0)

    parts = pl.pallas_call(
        project_kernel,
        grid_spec=pltpu.PrefetchScalarGridSpec(
            num_scalar_prefetch=1,
            grid=(groups,),
            in_specs=[whole(rows, channels), pl.BlockSpec((channels, channels), weight_block)],
            out_specs=[pl.BlockSpec((1, rows, channels), out_block(turn)) for turn in range(ring)],
        ),
        out_shape=[shape((2, rows, channels), BF16)] * ring,
        compiler_params=params(52),
        name="project",
    )(spot, gated, out_weight)
    parts = [
        lax.ppermute(part, "ch", [(i, (i + 2 * ahead) % groups) for i in range(groups)]) if ahead else part
        for part, ahead in zip(parts, order)
    ]
    far = sum(part[1].astype(F32) for part in parts).astype(BF16)
    near = sum(part[0].astype(F32) for part in parts)
    far = lax.ppermute(far, "ch", [(i, i ^ 1) for i in range(groups)])
    block_output = (near + far.astype(F32)).astype(BF16)

    columns = columns.reshape(shards * rows, width)
    summed = lax.dot_general(gated_all, columns, (((0,), (0,)), ((), ())), preferred_element_type=F32)
    weight_grad = (summed * scale).astype(BF16)
    return (block_output, gate_grad, value_grad, filter_grad, weight_grad)


def solution(mesh):
    placed = (P("seq", "ch"), P("seq", "ch"), P("seq", "ch"), P("ch", None), P("seq", "ch"))
    return jax.shard_map(
        body,
        mesh=mesh,
        in_specs=placed,
        out_specs=(P("seq", "ch"), P("seq", "ch"), P("seq", "ch"), P("seq", "ch"), P("ch", "seq")),
        check_vma=False,
    )
```

```python
import functools
import math

import jax
import jax.numpy as jnp
import numpy as np
from jax import lax
from jax.experimental import pallas as pl
from jax.experimental.pallas import tpu as pltpu
from jax.sharding import PartitionSpec as P

BLOCKS = 16
INNER = 128
PERIOD = 2 * BLOCKS * INNER
HALF = 64
GROUP = 16
BF16 = jnp.bfloat16
F32 = jnp.float32


def plane_order():
    order = [(0, False), (BLOCKS, False)]
    for freq in range(1, BLOCKS):
        order += [(freq, False), (freq, True)]
    return order


def outer_matrices():
    blocks = np.arange(BLOCKS)
    forward = np.zeros((2 * BLOCKS, BLOCKS))
    inverse = np.zeros((BLOCKS, 2 * BLOCKS))
    for plane, (freq, imaginary) in enumerate(plane_order()):
        turn = 2.0 * np.pi * ((freq * blocks) % (2 * BLOCKS)) / (2 * BLOCKS)
        weight = (1.0 if freq in (0, BLOCKS) else 2.0) / PERIOD
        wave = -np.sin(turn) if imaginary else np.cos(turn)
        forward[plane] = wave
        inverse[:, plane] = weight * wave
    eye = np.eye(GROUP)
    return np.kron(forward, eye), np.kron(inverse, eye)


def inner_matrices():
    freqs = np.arange(BLOCKS + 1)[:, None, None] + 2 * BLOCKS * np.arange(INNER)[None, :, None]
    turn = 2.0 * np.pi * ((freqs * np.arange(INNER)[None, None, :]) % PERIOD) / PERIOD
    cos, sin = np.cos(turn), np.sin(turn)
    back = [np.swapaxes(wave, 1, 2) for wave in (cos, sin)]
    return np.concatenate([cos, sin], axis=1), np.concatenate(back, axis=1)


def dot(left, right):
    return jnp.dot(left, right, preferred_element_type=F32)


def lane_low(shape):
    return lax.broadcasted_iota(jnp.int32, shape, len(shape) - 1) < HALF


def swap(array):
    return pltpu.roll(array, HALF, array.ndim - 1)


def pack_kernel(value_ref, taps_ref, out_ref):
    for pair in range(value_ref.shape[1] // INNER):
        lanes = pl.ds(pair * INNER, INNER)
        value = value_ref[:, lanes].astype(F32)
        taps = taps_ref[:, lanes]
        low = lane_low(value.shape)
        out_ref[2 * pair] = jnp.where(low, value, swap(taps)).astype(BF16)
        out_ref[2 * pair + 1] = jnp.where(low, swap(value), taps).astype(BF16)


def fold_rows(block):
    top, bottom = block[:HALF], block[HALF:]
    low = lane_low(top.shape)
    return jnp.where(low, top, swap(bottom)), jnp.where(low, swap(top), bottom)


def unfold_rows(first, second):
    low = lane_low(first.shape)
    return jnp.concatenate([jnp.where(low, first, swap(second)), jnp.where(low, swap(first), second)], 0)


def side_by_side(table_ref, first, count):
    return jnp.concatenate([table_ref[first + i] for i in range(count)], 1)


def outer_forward(read_group, table_ref, planes_ref):
    start = 2 * (BLOCKS + 1)
    for group in range(INNER // GROUP):
        rows = pl.ds(group * GROUP, GROUP)
        block = read_group(rows).reshape(BLOCKS * GROUP, INNER)
        for half in range(2):
            wide = dot(side_by_side(table_ref, start + 2 * half, 2), block).astype(BF16)
            planes_ref[pl.ds(half * BLOCKS, BLOCKS), rows, :] = wide.reshape(BLOCKS, GROUP, INNER)


def inner_forward(freq, table_ref, planes_ref):
    if freq in (0, BLOCKS):
        both = dot(table_ref[freq], planes_ref[0 if freq == 0 else 1])
        return both[:INNER], -both[INNER:]
    both = dot(table_ref[freq], jnp.concatenate([planes_ref[2 * freq], planes_ref[2 * freq + 1]], 1))
    return both[:INNER, :INNER] + both[INNER:, INNER:], both[:INNER, INNER:] - both[INNER:, :INNER]


def inner_inverse(freq, re, im, table_ref, planes_ref):
    both = dot(table_ref[BLOCKS + 1 + freq], jnp.concatenate([re.astype(BF16), im.astype(BF16)], 1))
    back_re = (both[:INNER, :INNER] - both[INNER:, INNER:]).astype(BF16)
    if freq in (0, BLOCKS):
        planes_ref[0 if freq == 0 else 1] = back_re
    else:
        planes_ref[2 * freq] = back_re
        planes_ref[2 * freq + 1] = (both[INNER:, :INNER] + both[:INNER, INNER:]).astype(BF16)


def outer_inverse(group, table_ref, planes_ref):
    planes = planes_ref[:, pl.ds(group * GROUP, GROUP), :].reshape(2 * BLOCKS * GROUP, INNER)
    return dot(side_by_side(table_ref, 2 * (BLOCKS + 1) + 4, 4), planes).reshape(BLOCKS, GROUP, INNER)


def transform_table():
    outer, outer_back = outer_matrices()
    blocks = list(inner_matrices())
    for half in range(2):
        rows = outer[half * 2 * INNER : (half + 1) * 2 * INNER]
        blocks.append(np.stack([rows[:, :INNER], rows[:, INNER:]]))
    blocks.append(np.stack(np.split(outer_back, 4, axis=1)))
    return np.concatenate(blocks)


def convolve_kernel(pair_ref, table_ref, out_ref, spec_hbm, spec_ref, planes_ref, back_ref, semaphore):
    outer_forward(lambda rows: pair_ref[:, rows, :], table_ref, planes_ref)
    for freq in range(BLOCKS + 1):
        re, im = inner_forward(freq, table_ref, planes_ref)
        spec_ref[freq, :INNER] = re.astype(BF16)
        spec_ref[freq, INNER:] = im.astype(BF16)
        other_re, other_im = swap(re), swap(im)
        inner_inverse(freq, re * other_re - im * other_im, re * other_im + im * other_re, table_ref, back_ref)
    send = pltpu.make_async_copy(spec_ref, spec_hbm, semaphore)
    send.start()
    half_groups = INNER // GROUP // 2
    for group in range(half_groups):
        one = outer_inverse(group, table_ref, back_ref)
        two = outer_inverse(group + half_groups, table_ref, back_ref)
        packed = jnp.where(lane_low(one.shape), one, two)
        out_ref[:, pl.ds(group * GROUP, GROUP), :] = packed.astype(BF16)
    send.wait()


def correlate_kernel(grad_ref, spec_hbm, table_ref, out_ref, spec_ref, wide_ref, planes_ref, back_ref, semaphore):
    load = pltpu.make_async_copy(spec_hbm, spec_ref, semaphore)
    load.start()
    for block in range(BLOCKS):
        packed = grad_ref[block].astype(F32)
        turned = swap(packed)
        low = lane_low(packed.shape)
        wide_ref[block, :HALF] = jnp.where(low, packed, turned).astype(BF16)
        wide_ref[block, HALF:] = jnp.where(low, turned, packed).astype(BF16)
    outer_forward(lambda rows: wide_ref[:, rows, :], table_ref, planes_ref)
    load.wait()
    for freq in range(BLOCKS + 1):
        grad_re, grad_im = inner_forward(freq, table_ref, planes_ref)
        re, im = spec_ref[freq, :INNER].astype(F32), spec_ref[freq, INNER:].astype(F32)
        inner_inverse(freq, re * grad_re + im * grad_im, re * grad_im - im * grad_re, table_ref, back_ref)
    for group in range(INNER // GROUP):
        out_ref[:, pl.ds(group * GROUP, GROUP), :] = outer_inverse(group, table_ref, back_ref).astype(BF16)


def fetch(pairs, semaphores):
    copies = [pltpu.make_async_copy(source, target, semaphores.at[i]) for i, (source, target) in enumerate(pairs)]
    for copy in copies:
        copy.start()
    return copies


def gate_kernel(recv_ref, gate_ref, conv_ref, gated_ref):
    for pair in range(BLOCKS // 2):
        conv = unfold_rows(recv_ref[2 * pair].astype(F32), recv_ref[2 * pair + 1].astype(F32))
        lanes = pl.ds(pair * INNER, INNER)
        conv_ref[:, lanes] = conv
        gated_ref[:, lanes] = (gate_ref[:, lanes].astype(F32) * conv).astype(BF16)


def finish_kernel(scale, recv_ref, value_grad_ref, filter_grad_ref):
    for pair in range(BLOCKS // 2):
        first = recv_ref[2 * pair].astype(F32)
        second = recv_ref[2 * pair + 1].astype(F32)
        low = lane_low(first.shape)
        lanes = pl.ds(pair * INNER, INNER)
        filter_grad_ref[:, lanes] = jnp.where(low, first, swap(second)) * scale
        value_grad_ref[:, lanes] = jnp.where(low, swap(first), second).astype(BF16)


def stream_weight(weight_hbm, block_column, buffers, semaphores, count, use):
    depth, _, width = buffers.shape

    def copy(step):
        columns = pl.ds(pl.multiple_of(block_column(step) * width, width), width)
        return pltpu.make_async_copy(weight_hbm.at[:, columns], buffers.at[step % depth], semaphores.at[step % depth])

    for step in range(depth - 1):
        copy(step).start()
    for step in range(count):
        if step + depth - 1 < count:
            copy(step + depth - 1).start()
        copy(step).wait()
        use(step, buffers.at[step % depth])


def grad_column(spot_ref, block):
    return block // 2 * 2 + lax.rem(spot_ref[1] + block % 2, 2)


def columns_kernel(spot_ref, grad_ref, out_ref):
    blocks, rows, channels = grad_ref.shape
    split = channels // 4
    quarter = rows // 4
    part = pl.ds(pl.multiple_of(spot_ref[0] * quarter, quarter), quarter)
    for block in range(blocks):
        for half in range(2):
            target = 2 * grad_column(spot_ref, block) + half
            start = 2 * half * split
            out_ref[target, :rows] = grad_ref[block, :, start : start + split]
            out_ref[target, rows:] = grad_ref[block, part, start + split : start + 2 * split]


def pre_grad_kernel(spot_ref, grad_ref, weight_hbm, gate_ref, total_ref, cotangent_ref, buffers, semaphores):
    def use(step, weight):
        part = lax.dot_general(grad_ref[step], weight[...], (((1,), (1,)), ((), ())), preferred_element_type=F32)
        total_ref[...] = part if step == 0 else total_ref[...] + part

    column = functools.partial(grad_column, spot_ref)
    stream_weight(weight_hbm, column, buffers, semaphores, grad_ref.shape[0], use)
    for pair in range(BLOCKS // 2):
        lanes = pl.ds(pair * INNER, INNER)
        first, second = fold_rows(total_ref[:, lanes] * gate_ref[:, lanes].astype(F32))
        cotangent_ref[2 * pair] = first.astype(BF16)
        cotangent_ref[2 * pair + 1] = second.astype(BF16)


def project_kernel(order, spot_ref, gated_ref, weight_hbm, *refs):
    out_refs, (buffers, semaphores) = refs[: len(order)], refs[len(order) :]
    depth, side = spot_ref[0], spot_ref[1]

    def column(step):
        layer = lax.rem(depth + order[step // 2], len(order))
        return 2 * layer + (side if step % 2 == 0 else 1 - side)

    def use(step, weight):
        out_refs[step // 2][step % 2] = dot(gated_ref[...], weight[...]).astype(BF16)

    stream_weight(weight_hbm, column, buffers, semaphores, 2 * len(order), use)


def weight_grad_kernel(scale, spot_ref, gated_ref, columns_hbm, far1_hbm, far2_hbm, far3_hbm, out_ref, wide_ref, semaphores):
    count, rows, width = wide_ref.shape
    split = width // 2
    quarter = rows // 4

    @pl.when(pl.program_id(0) == 0)
    def _():
        moves = [(columns_hbm.at[:, pl.ds(0, rows)], wide_ref.at[:, :, pl.ds(0, split)])]
        sources = (columns_hbm.at[:, pl.ds(rows, quarter)], far1_hbm, far2_hbm, far3_hbm)
        for back, source in enumerate(sources):
            layer = lax.rem(spot_ref[0] + 4 - back, 4)
            part = pl.ds(pl.multiple_of(layer * quarter, quarter), quarter)
            moves.append((source, wide_ref.at[:, part, pl.ds(split, split)]))
        for copy in fetch(moves, semaphores):
            copy.wait()

    columns = wide_ref[...].reshape(count * rows, width)
    total = lax.dot_general(gated_ref[...], columns, (((0,), (0,)), ((), ())), preferred_element_type=F32)
    out_ref[...] = (total * scale).astype(BF16)


def shape(dims, kind):
    return jax.ShapeDtypeStruct(dims, kind)


def params(mebibytes=16):
    return pltpu.CompilerParams(vmem_limit_bytes=mebibytes * 1024 * 1024)


def after(array, other):
    return lax.optimization_barrier((array, other))[0]


def exchange(array, axis, groups=None):
    return lax.all_to_all(array, axis, split_axis=0, concat_axis=0, tiled=True, axis_index_groups=groups)


def cost(microseconds):
    return pl.CostEstimate(flops=0, bytes_accessed=int(microseconds * 3.5e6), transcendentals=0)


def body(gate_input, value_input, filter_taps, out_weight, grad_output):
    rows, channels = gate_input.shape
    shards = lax.axis_size("seq")
    groups = lax.axis_size("ch")
    scale = 1.0 / math.sqrt(rows * shards)
    width = channels * groups // shards
    table = jnp.asarray(transform_table(), BF16)
    planes = pltpu.VMEM((2 * BLOCKS, INNER, INNER), BF16)
    spectra = pltpu.VMEM((BLOCKS + 1, 2 * INNER, INNER), BF16)
    anywhere = pl.BlockSpec(memory_space=pl.ANY)
    vmem = pl.BlockSpec(memory_space=pltpu.VMEM)
    smem = pl.BlockSpec(memory_space=pltpu.SMEM)
    place = lax.axis_index("ch")
    ring = groups // 2
    spot = jnp.stack([place // 2, place % 2]).astype(jnp.int32)
    ahead_by = lambda ahead: [(i, (i + 2 * ahead) % groups) for i in range(groups)]
    across = [(i, i ^ 1) for i in range(groups)]
    layers = [[2 * i + j for i in range(ring)] for j in range(2)]

    partner = lax.ppermute(grad_output, "ch", across)
    pair = pl.pallas_call(
        pack_kernel,
        out_shape=shape((shards, rows, INNER), BF16),
        compiler_params=params(60),
        cost_estimate=cost(2),
        name="pack",
    )(value_input, filter_taps)
    partner = after(partner, pair)
    sides = jnp.stack([grad_output, partner])
    grad_full = lax.all_gather(sides, "ch", axis=0, tiled=True, axis_index_groups=layers)
    pair = exchange(pair, "seq")
    packed, spec = pl.pallas_call(
        convolve_kernel,
        out_specs=(vmem, anywhere),
        out_shape=(shape((shards, HALF, INNER), BF16), shape((BLOCKS + 1, 2 * INNER, INNER), BF16)),
        scratch_shapes=[spectra, planes, planes, pltpu.SemaphoreType.DMA],
        compiler_params=params(16),
        cost_estimate=cost(3),
        name="convolve",
    )(pair, table)
    conv, gated = pl.pallas_call(
        gate_kernel,
        out_shape=(shape((rows, channels), F32), shape((rows, channels), BF16)),
        compiler_params=params(),
        cost_estimate=cost(1),
        name="gate",
    )(exchange(packed, "seq"), gate_input)

    gated_all = lax.all_gather(gated, "seq", axis=0, tiled=True)
    split, quarter = width // 2, rows // ring
    columns = pl.pallas_call(
        columns_kernel,
        in_specs=[smem, vmem],
        out_shape=shape((shards, rows + quarter, split), BF16),
        compiler_params=params(60),
        cost_estimate=cost(2),
        name="columns",
    )(spot, grad_full)
    columns = exchange(after(columns, gated), "seq")

    stream_scratch = [pltpu.VMEM((4, channels, channels), BF16), pltpu.SemaphoreType.DMA((4,))]
    pre_grad, cotangent = pl.pallas_call(
        pre_grad_kernel,
        in_specs=[smem, vmem, anywhere, vmem],
        out_shape=(shape((rows, channels), F32), shape((shards, HALF, INNER), BF16)),
        scratch_shapes=stream_scratch,
        compiler_params=params(50),
        cost_estimate=cost(9),
        name="pre_grad",
    )(spot, grad_full, out_weight, gate_input)
    gate_grad = (pre_grad * conv).astype(BF16)

    order = (2, 1, 3, 0)
    parts = pl.pallas_call(
        functools.partial(project_kernel, order),
        in_specs=[smem, vmem, anywhere],
        out_shape=[shape((2, rows, channels), BF16)] * ring,
        scratch_shapes=stream_scratch,
        compiler_params=params(50),
        cost_estimate=cost(8),
        name="project",
    )(spot, gated, out_weight)
    parts = [lax.ppermute(part, "ch", ahead_by(ahead)) if ahead else part for part, ahead in zip(parts, order)]

    part = columns[:, rows:]
    shared = [lax.ppermute(part, "ch", ahead_by(ahead)) for ahead in (1, 2, 3)]
    parts = [after(got, (columns, cotangent)) for got in parts]
    cotangent = exchange(after(cotangent, (columns, gate_grad)), "seq")
    returned = pl.pallas_call(
        correlate_kernel,
        out_shape=shape((shards, rows, INNER), BF16),
        in_specs=[vmem, anywhere, vmem],
        scratch_shapes=[spectra, pltpu.VMEM((shards, rows, INNER), BF16), planes, planes, pltpu.SemaphoreType.DMA],
        compiler_params=params(16),
        cost_estimate=cost(3),
        name="correlate",
    )(after(cotangent, tuple(parts)), spec, table)

    parts = [after(got, returned) for got in parts]
    opposite = sum(part[1].astype(F32) for part in parts).astype(BF16)
    kept = sum(part[0].astype(F32) for part in parts)
    returned = exchange(returned, "seq")

    opposite = lax.ppermute(opposite, "ch", across)

    weight_grad = pl.pallas_call(
        functools.partial(weight_grad_kernel, scale),
        grid=(4,),
        in_specs=[smem, pl.BlockSpec((shards * rows, channels // 4), lambda step: (0, step))] + [anywhere] * ring,
        out_specs=pl.BlockSpec((channels // 4, width), lambda step: (step, 0)),
        out_shape=shape((channels, width), BF16),
        scratch_shapes=[pltpu.VMEM((shards, rows, width), BF16), pltpu.SemaphoreType.DMA((ring + 1,))],
        compiler_params=params(60),
        cost_estimate=cost(6),
        name="weight_grad",
    )(spot, gated_all, columns, *shared)
    value_grad, filter_grad = pl.pallas_call(
        functools.partial(finish_kernel, scale),
        out_shape=(shape((rows, channels), BF16), shape((rows, channels), F32)),
        compiler_params=params(),
        cost_estimate=cost(1),
        name="finish",
    )(after(returned, weight_grad))
    opposite = after(opposite, weight_grad)
    block_output = (kept + opposite.astype(F32)).astype(BF16)
    return (block_output, gate_grad, value_grad, filter_grad, weight_grad)


def solution(mesh):
    placed = (P("seq", "ch"), P("seq", "ch"), P("seq", "ch"), P("ch", None), P("seq", "ch"))
    return jax.shard_map(
        body,
        mesh=mesh,
        in_specs=placed,
        out_specs=(P("seq", "ch"), P("seq", "ch"), P("seq", "ch"), P("seq", "ch"), P("ch", "seq")),
        check_vma=False,
    )
```

```python
import functools
import math

import jax
import jax.numpy as jnp
import numpy as np
from jax import lax
from jax.experimental import pallas as pl
from jax.experimental.pallas import tpu as pltpu
from jax.sharding import PartitionSpec as P

BLOCKS = 16
INNER = 128
PERIOD = 2 * BLOCKS * INNER
HALF = 64
GROUP = 16
BF16 = jnp.bfloat16
F32 = jnp.float32


def plane_order():
    order = [(0, False), (BLOCKS, False)]
    for freq in range(1, BLOCKS):
        order += [(freq, False), (freq, True)]
    return order


def outer_matrices():
    blocks = np.arange(BLOCKS)
    forward = np.zeros((2 * BLOCKS, BLOCKS))
    inverse = np.zeros((BLOCKS, 2 * BLOCKS))
    for plane, (freq, imaginary) in enumerate(plane_order()):
        turn = 2.0 * np.pi * ((freq * blocks) % (2 * BLOCKS)) / (2 * BLOCKS)
        weight = (1.0 if freq in (0, BLOCKS) else 2.0) / PERIOD
        wave = -np.sin(turn) if imaginary else np.cos(turn)
        forward[plane] = wave
        inverse[:, plane] = weight * wave
    eye = np.eye(GROUP)
    return np.kron(forward, eye), np.kron(inverse, eye)


def inner_matrices():
    freqs = np.arange(BLOCKS + 1)[:, None, None] + 2 * BLOCKS * np.arange(INNER)[None, :, None]
    turn = 2.0 * np.pi * ((freqs * np.arange(INNER)[None, None, :]) % PERIOD) / PERIOD
    cos, sin = np.cos(turn), np.sin(turn)
    back = [np.swapaxes(wave, 1, 2) for wave in (cos, sin)]
    return np.concatenate([cos, sin], axis=1), np.concatenate(back, axis=1)


def dot(left, right):
    return jnp.dot(left, right, preferred_element_type=F32)


def lane_low(shape):
    return lax.broadcasted_iota(jnp.int32, shape, len(shape) - 1) < HALF


def swap(array):
    return pltpu.roll(array, HALF, array.ndim - 1)


def pack_kernel(value_ref, taps_ref, out_ref):
    for pair in range(value_ref.shape[1] // INNER):
        lanes = pl.ds(pair * INNER, INNER)
        value = value_ref[:, lanes].astype(F32)
        taps = taps_ref[:, lanes]
        low = lane_low(value.shape)
        out_ref[2 * pair] = jnp.where(low, value, swap(taps)).astype(BF16)
        out_ref[2 * pair + 1] = jnp.where(low, swap(value), taps).astype(BF16)


def fold_rows(block):
    top, bottom = block[:HALF], block[HALF:]
    low = lane_low(top.shape)
    return jnp.where(low, top, swap(bottom)), jnp.where(low, swap(top), bottom)


def unfold_rows(first, second):
    low = lane_low(first.shape)
    return jnp.concatenate([jnp.where(low, first, swap(second)), jnp.where(low, swap(first), second)], 0)


def side_by_side(table_ref, first, count):
    return jnp.concatenate([table_ref[first + i] for i in range(count)], 1)


def outer_forward(read_group, table_ref, planes_ref):
    start = 2 * (BLOCKS + 1)
    for group in range(INNER // GROUP):
        rows = pl.ds(group * GROUP, GROUP)
        block = read_group(rows).reshape(BLOCKS * GROUP, INNER)
        for half in range(2):
            wide = dot(side_by_side(table_ref, start + 2 * half, 2), block).astype(BF16)
            planes_ref[pl.ds(half * BLOCKS, BLOCKS), rows, :] = wide.reshape(BLOCKS, GROUP, INNER)


def inner_forward(freq, table_ref, planes_ref):
    if freq in (0, BLOCKS):
        both = dot(table_ref[freq], planes_ref[0 if freq == 0 else 1])
        return both[:INNER], -both[INNER:]
    both = dot(table_ref[freq], jnp.concatenate([planes_ref[2 * freq], planes_ref[2 * freq + 1]], 1))
    return both[:INNER, :INNER] + both[INNER:, INNER:], both[:INNER, INNER:] - both[INNER:, :INNER]


def inner_inverse(freq, re, im, table_ref, planes_ref):
    both = dot(table_ref[BLOCKS + 1 + freq], jnp.concatenate([re.astype(BF16), im.astype(BF16)], 1))
    back_re = (both[:INNER, :INNER] - both[INNER:, INNER:]).astype(BF16)
    if freq in (0, BLOCKS):
        planes_ref[0 if freq == 0 else 1] = back_re
    else:
        planes_ref[2 * freq] = back_re
        planes_ref[2 * freq + 1] = (both[INNER:, :INNER] + both[:INNER, INNER:]).astype(BF16)


def outer_inverse(group, table_ref, planes_ref):
    planes = planes_ref[:, pl.ds(group * GROUP, GROUP), :].reshape(2 * BLOCKS * GROUP, INNER)
    return dot(side_by_side(table_ref, 2 * (BLOCKS + 1) + 4, 4), planes).reshape(BLOCKS, GROUP, INNER)


def transform_table():
    outer, outer_back = outer_matrices()
    blocks = list(inner_matrices())
    for half in range(2):
        rows = outer[half * 2 * INNER : (half + 1) * 2 * INNER]
        blocks.append(np.stack([rows[:, :INNER], rows[:, INNER:]]))
    blocks.append(np.stack(np.split(outer_back, 4, axis=1)))
    return np.concatenate(blocks)


def convolve_kernel(pair_ref, table_ref, out_ref, spec_hbm, spec_ref, planes_ref, back_ref, semaphore):
    outer_forward(lambda rows: pair_ref[:, rows, :], table_ref, planes_ref)
    for freq in range(BLOCKS + 1):
        re, im = inner_forward(freq, table_ref, planes_ref)
        spec_ref[freq, :INNER] = re.astype(BF16)
        spec_ref[freq, INNER:] = im.astype(BF16)
        other_re, other_im = swap(re), swap(im)
        inner_inverse(freq, re * other_re - im * other_im, re * other_im + im * other_re, table_ref, back_ref)
    send = pltpu.make_async_copy(spec_ref, spec_hbm, semaphore)
    send.start()
    half_groups = INNER // GROUP // 2
    for group in range(half_groups):
        one = outer_inverse(group, table_ref, back_ref)
        two = outer_inverse(group + half_groups, table_ref, back_ref)
        packed = jnp.where(lane_low(one.shape), one, two)
        out_ref[:, pl.ds(group * GROUP, GROUP), :] = packed.astype(BF16)
    send.wait()


def correlate_kernel(grad_ref, spec_hbm, table_ref, out_ref, spec_ref, wide_ref, planes_ref, back_ref, semaphore):
    load = pltpu.make_async_copy(spec_hbm, spec_ref, semaphore)
    load.start()
    for block in range(BLOCKS):
        packed = grad_ref[block].astype(F32)
        turned = swap(packed)
        low = lane_low(packed.shape)
        wide_ref[block, :HALF] = jnp.where(low, packed, turned).astype(BF16)
        wide_ref[block, HALF:] = jnp.where(low, turned, packed).astype(BF16)
    outer_forward(lambda rows: wide_ref[:, rows, :], table_ref, planes_ref)
    load.wait()
    for freq in range(BLOCKS + 1):
        grad_re, grad_im = inner_forward(freq, table_ref, planes_ref)
        re, im = spec_ref[freq, :INNER].astype(F32), spec_ref[freq, INNER:].astype(F32)
        inner_inverse(freq, re * grad_re + im * grad_im, re * grad_im - im * grad_re, table_ref, back_ref)
    for group in range(INNER // GROUP):
        out_ref[:, pl.ds(group * GROUP, GROUP), :] = outer_inverse(group, table_ref, back_ref).astype(BF16)


def fetch(pairs, semaphores):
    copies = [pltpu.make_async_copy(source, target, semaphores.at[i]) for i, (source, target) in enumerate(pairs)]
    for copy in copies:
        copy.start()
    return copies


def gate_kernel(recv_ref, gate_ref, pre_ref, gated_ref, gate_grad_ref):
    for pair in range(BLOCKS // 2):
        conv = unfold_rows(recv_ref[2 * pair].astype(F32), recv_ref[2 * pair + 1].astype(F32))
        lanes = pl.ds(pair * INNER, INNER)
        gated_ref[:, lanes] = (gate_ref[:, lanes].astype(F32) * conv).astype(BF16)
        gate_grad_ref[:, lanes] = (pre_ref[:, lanes] * conv).astype(BF16)


def finish_kernel(scale, recv_ref, value_grad_ref, filter_grad_ref):
    for pair in range(BLOCKS // 2):
        first = recv_ref[2 * pair].astype(F32)
        second = recv_ref[2 * pair + 1].astype(F32)
        low = lane_low(first.shape)
        lanes = pl.ds(pair * INNER, INNER)
        filter_grad_ref[:, lanes] = jnp.where(low, first, swap(second)) * scale
        value_grad_ref[:, lanes] = jnp.where(low, swap(first), second).astype(BF16)


def stream_weight(weight_hbm, block_column, buffers, semaphores, count, use):
    depth, _, width = buffers.shape

    def copy(step):
        columns = pl.ds(pl.multiple_of(block_column(step) * width, width), width)
        return pltpu.make_async_copy(weight_hbm.at[:, columns], buffers.at[step % depth], semaphores.at[step % depth])

    for step in range(depth - 1):
        copy(step).start()
    for step in range(count):
        if step + depth - 1 < count:
            copy(step + depth - 1).start()
        copy(step).wait()
        use(step, buffers.at[step % depth])


DIRECT = 1


def column_rows(piece):
    if piece < DIRECT:
        return HALF + piece * INNER, INNER
    return HALF + DIRECT * INNER + (piece - DIRECT) * HALF, HALF


def gathered_block(spot_ref, step):
    depth, side = spot_ref[0], spot_ref[1]
    if step < 4:
        return 2 * step + side
    return 2 * lax.rem(depth + 8 - step, 4) + 1 - side


def pre_grad_kernel(spot_ref, near_ref, far0_ref, far1_ref, far2_ref, far3_ref, weight_hbm, gate_ref, *refs):
    total_ref, send_ref, buffers, semaphores = refs
    ring, rows, channels = near_ref.shape
    far = (far0_ref, far1_ref, far2_ref, far3_ref)
    upper = pl.ds(pl.multiple_of(lax.rem(spot_ref[0], 2) * HALF, HALF), HALF)

    def use(step, weight):
        block_ref = near_ref.at[step] if step < ring else far[step - ring]
        part = lax.dot_general(block_ref[...], weight[...], (((1,), (1,)), ((), ())), preferred_element_type=F32)
        total_ref[...] = part if step == 0 else total_ref[...] + part
        for half in range(2):
            target = 2 * gathered_block(spot_ref, step) + half
            start = half * (channels // 2)
            for piece in range(4):
                lanes = pl.ds(start + piece * INNER, INNER)
                place, size = column_rows(piece)
                send_ref[target, pl.ds(place, size)] = block_ref[:, lanes] if piece < DIRECT else block_ref[upper, lanes]

    stream_weight(weight_hbm, functools.partial(gathered_block, spot_ref), buffers, semaphores, 2 * ring, use)
    for pair in range(BLOCKS // 2):
        lanes = pl.ds(pair * INNER, INNER)
        first, second = fold_rows(total_ref[:, lanes] * gate_ref[:, lanes].astype(F32))
        send_ref[2 * pair, :HALF] = first.astype(BF16)
        send_ref[2 * pair + 1, :HALF] = second.astype(BF16)


def project_kernel(order, spot_ref, gated_ref, weight_hbm, *refs):
    out_refs, (buffers, semaphores) = refs[: len(order)], refs[len(order) :]
    depth, side = spot_ref[0], spot_ref[1]

    def column(step):
        layer = lax.rem(depth + order[step // 2], len(order))
        return 2 * layer + (side if step % 2 == 0 else 1 - side)

    def use(step, weight):
        out_refs[step // 2][step % 2] = dot(gated_ref[...], weight[...]).astype(BF16)

    stream_weight(weight_hbm, column, buffers, semaphores, 2 * len(order), use)


def weight_grad_kernel(scale, spot_ref, gated_hbm, received_hbm, shared_hbm, out_ref, gated_ref, wide_ref, total_ref, arrived, semaphores):
    parts = gated_ref.shape[0]
    side = lax.rem(spot_ref[0], 2)
    own = pl.ds(pl.multiple_of(side * HALF, HALF), HALF)
    other = pl.ds(pl.multiple_of((1 - side) * HALF, HALF), HALF)
    moves = []
    for piece in range(4):
        lanes = pl.ds(piece * INNER, INNER)
        place, size = column_rows(piece)
        source = received_hbm.at[:, pl.ds(place, size)]
        if piece < DIRECT:
            moves.append((source, wide_ref.at[:, :, lanes]))
        else:
            moves.append((source, wide_ref.at[:, own, lanes]))
            part = pl.ds((piece - DIRECT) * HALF, HALF)
            moves.append((shared_hbm.at[:, part], wide_ref.at[:, other, lanes]))
    copies = fetch(moves, semaphores)
    loads = fetch([(gated_hbm.at[part], gated_ref.at[part]) for part in range(parts)], arrived)
    for copy in copies:
        copy.wait()
    count, rows, width = wide_ref.shape
    tile = out_ref.shape[0] // 4
    for part in range(parts):
        loads[part].wait()
        columns = wide_ref[part * count // parts : (part + 1) * count // parts].reshape(-1, width)
        for first in range(0, out_ref.shape[0], tile):
            place = pl.ds(first, tile)
            total = lax.dot_general(
                gated_ref[part, :, place], columns, (((0,), (0,)), ((), ())), preferred_element_type=F32
            )
            if part > 0:
                total += total_ref[place]
            if part < parts - 1:
                total_ref[place] = total
            else:
                out_ref[place] = (total * scale).astype(BF16)


def add_kernel(kept_ref, other_ref, out_ref):
    out_ref[...] = (kept_ref[...] + other_ref[...].astype(F32)).astype(BF16)


def shape(dims, kind):
    return jax.ShapeDtypeStruct(dims, kind)


def params(mebibytes=16):
    return pltpu.CompilerParams(vmem_limit_bytes=mebibytes * 1024 * 1024)


def after(array, other):
    return lax.optimization_barrier((array, other))[0]


def exchange(array, axis, groups=None):
    return lax.all_to_all(array, axis, split_axis=0, concat_axis=0, tiled=True, axis_index_groups=groups)


def cost(microseconds):
    return pl.CostEstimate(flops=0, bytes_accessed=int(microseconds * 3.5e6), transcendentals=0)


def body(gate_input, value_input, filter_taps, out_weight, grad_output):
    rows, channels = gate_input.shape
    shards = lax.axis_size("seq")
    groups = lax.axis_size("ch")
    scale = 1.0 / math.sqrt(rows * shards)
    width = channels * groups // shards
    table = jnp.asarray(transform_table(), BF16)
    planes = pltpu.VMEM((2 * BLOCKS, INNER, INNER), BF16)
    spectra = pltpu.VMEM((BLOCKS + 1, 2 * INNER, INNER), BF16)
    anywhere = pl.BlockSpec(memory_space=pl.ANY)
    vmem = pl.BlockSpec(memory_space=pltpu.VMEM)
    smem = pl.BlockSpec(memory_space=pltpu.SMEM)
    place = lax.axis_index("ch")
    ring = groups // 2
    spot = jnp.stack([place // 2, place % 2]).astype(jnp.int32)
    ahead_by = lambda ahead: [(i, (i + 2 * ahead) % groups) for i in range(groups)]
    across = [(i, i ^ 1) for i in range(groups)]
    layers = [[2 * i + j for i in range(ring)] for j in range(2)]

    partner = lax.ppermute(grad_output, "ch", across)
    pair = pl.pallas_call(
        pack_kernel,
        out_shape=shape((shards, rows, INNER), BF16),
        compiler_params=params(60),
        cost_estimate=cost(2),
        name="pack",
    )(value_input, filter_taps)
    near = lax.all_gather(grad_output, "ch", axis=0, tiled=False, axis_index_groups=layers)
    far = [after(partner, pair)]
    far += [lax.ppermute(far[0], "ch", ahead_by(ahead)) for ahead in (1, 2, 3)]
    pair = exchange(after(pair, partner), "seq")
    packed, spec = pl.pallas_call(
        convolve_kernel,
        out_specs=(vmem, anywhere),
        out_shape=(shape((shards, HALF, INNER), BF16), shape((BLOCKS + 1, 2 * INNER, INNER), BF16)),
        scratch_shapes=[spectra, planes, planes, pltpu.SemaphoreType.DMA],
        compiler_params=params(16),
        cost_estimate=cost(3),
        name="convolve",
    )(pair, table)
    stream_scratch = [pltpu.VMEM((4, channels, channels), BF16), pltpu.SemaphoreType.DMA((4,))]
    direct = HALF + DIRECT * INNER
    depth = direct + (4 - DIRECT) * HALF
    pre_grad, send = pl.pallas_call(
        pre_grad_kernel,
        in_specs=[smem] + [vmem] * 5 + [anywhere, vmem],
        out_shape=(shape((rows, channels), F32), shape((shards, depth, INNER), BF16)),
        scratch_shapes=stream_scratch,
        compiler_params=params(50),
        cost_estimate=cost(9),
        name="pre_grad",
    )(spot, near, *far, out_weight, gate_input)
    gated, gate_grad = pl.pallas_call(
        gate_kernel,
        out_shape=[shape((rows, channels), BF16)] * 2,
        compiler_params=params(),
        cost_estimate=cost(1),
        name="gate",
    )(exchange(packed, "seq"), gate_input, pre_grad)

    gated_all = lax.all_gather(gated, "seq", axis=0, tiled=True)
    received = exchange(after(send, gated), "seq")

    order = (2, 1, 3, 0)
    parts = pl.pallas_call(
        functools.partial(project_kernel, order),
        in_specs=[smem, vmem, anywhere],
        out_shape=[shape((2, rows, channels), BF16)] * ring,
        scratch_shapes=stream_scratch,
        compiler_params=params(50),
        cost_estimate=cost(8),
        name="project",
    )(spot, gated, out_weight)
    parts = [lax.ppermute(part, "ch", ahead_by(ahead)) if ahead else part for part, ahead in zip(parts, order)]

    part = received[:, direct:]
    shared = lax.ppermute(part, "ch", [(i, i ^ 2) for i in range(groups)])
    returned = pl.pallas_call(
        correlate_kernel,
        grid=(1,),
        out_shape=shape((shards, rows, INNER), BF16),
        in_specs=[pl.BlockSpec((shards, HALF, INNER), lambda step: (0, 0, 0)), anywhere, vmem],
        out_specs=vmem,
        scratch_shapes=[spectra, pltpu.VMEM((shards, rows, INNER), BF16), planes, planes, pltpu.SemaphoreType.DMA],
        compiler_params=params(16),
        cost_estimate=cost(3),
        name="correlate",
    )(after(received, part), spec, table)

    parts = [after(got, returned) for got in parts]
    opposite = sum(part[1].astype(F32) for part in parts).astype(BF16)
    kept = sum(part[0].astype(F32) for part in parts)
    returned = exchange(returned, "seq")

    opposite = lax.ppermute(opposite, "ch", across)

    weight_grad = pl.pallas_call(
        functools.partial(weight_grad_kernel, scale),
        in_specs=[smem, anywhere, anywhere, anywhere],
        out_shape=shape((channels, width), BF16),
        scratch_shapes=[
            pltpu.VMEM((4, shards * rows // 4, channels), BF16),
            pltpu.VMEM((shards, rows, width), BF16),
            pltpu.VMEM((channels, width), F32),
            pltpu.SemaphoreType.DMA((4,)),
            pltpu.SemaphoreType.DMA((8 - DIRECT,)),
        ],
        compiler_params=params(60),
        cost_estimate=cost(6),
        name="weight_grad",
    )(spot, gated_all.reshape(4, shards * rows // 4, channels), received, shared)
    value_grad, filter_grad = pl.pallas_call(
        functools.partial(finish_kernel, scale),
        out_shape=(shape((rows, channels), BF16), shape((rows, channels), F32)),
        compiler_params=params(),
        cost_estimate=cost(1),
        name="finish",
    )(after(returned, weight_grad))
    opposite = after(opposite, (weight_grad, value_grad))
    block_output = pl.pallas_call(
        add_kernel,
        out_shape=shape((rows, channels), BF16),
        compiler_params=params(),
        cost_estimate=cost(1),
        name="add_opposite",
    )(kept, opposite)
    return (block_output, gate_grad, value_grad, filter_grad, weight_grad)


def solution(mesh):
    placed = (P("seq", "ch"), P("seq", "ch"), P("seq", "ch"), P("ch", None), P("seq", "ch"))
    return jax.shard_map(
        body,
        mesh=mesh,
        in_specs=placed,
        out_specs=(P("seq", "ch"), P("seq", "ch"), P("seq", "ch"), P("seq", "ch"), P("ch", "seq")),
        check_vma=False,
    )
```

```python
import functools
import math

import jax
import jax.numpy as jnp
import numpy as np
from jax import lax
from jax.experimental import pallas as pl
from jax.experimental.pallas import tpu as pltpu
from jax.sharding import PartitionSpec as P

BLOCKS = 16
INNER = 128
PERIOD = 2 * BLOCKS * INNER
HALF = 64
GROUP = 16
BF16 = jnp.bfloat16
F32 = jnp.float32


def plane_order():
    order = [(0, False), (BLOCKS, False)]
    for freq in range(1, BLOCKS):
        order += [(freq, False), (freq, True)]
    return order


def outer_matrices():
    blocks = np.arange(BLOCKS)
    forward = np.zeros((2 * BLOCKS, BLOCKS))
    inverse = np.zeros((BLOCKS, 2 * BLOCKS))
    for plane, (freq, imaginary) in enumerate(plane_order()):
        turn = 2.0 * np.pi * ((freq * blocks) % (2 * BLOCKS)) / (2 * BLOCKS)
        weight = (1.0 if freq in (0, BLOCKS) else 2.0) / PERIOD
        wave = -np.sin(turn) if imaginary else np.cos(turn)
        forward[plane] = wave
        inverse[:, plane] = weight * wave
    eye = np.eye(GROUP)
    return np.kron(forward, eye), np.kron(inverse, eye)


def inner_matrices():
    freqs = np.arange(BLOCKS + 1)[:, None, None] + 2 * BLOCKS * np.arange(INNER)[None, :, None]
    turn = 2.0 * np.pi * ((freqs * np.arange(INNER)[None, None, :]) % PERIOD) / PERIOD
    cos, sin = np.cos(turn), np.sin(turn)
    back = [np.swapaxes(wave, 1, 2) for wave in (cos, sin)]
    return np.concatenate([cos, sin], axis=1), np.concatenate(back, axis=1)


def dot(left, right):
    return jnp.dot(left, right, preferred_element_type=F32)


def lane_low(shape):
    return lax.broadcasted_iota(jnp.int32, shape, len(shape) - 1) < HALF


def swap(array):
    return pltpu.roll(array, HALF, array.ndim - 1)


def pack_kernel(value_ref, taps_ref, out_ref):
    for pair in range(value_ref.shape[1] // INNER):
        lanes = pl.ds(pair * INNER, INNER)
        value = value_ref[:, lanes].astype(F32)
        taps = taps_ref[:, lanes]
        low = lane_low(value.shape)
        out_ref[2 * pair] = jnp.where(low, value, swap(taps)).astype(BF16)
        out_ref[2 * pair + 1] = jnp.where(low, swap(value), taps).astype(BF16)


def fold_rows(block):
    top, bottom = block[:HALF], block[HALF:]
    low = lane_low(top.shape)
    return jnp.where(low, top, swap(bottom)), jnp.where(low, swap(top), bottom)


def unfold_rows(first, second):
    low = lane_low(first.shape)
    return jnp.concatenate([jnp.where(low, first, swap(second)), jnp.where(low, swap(first), second)], 0)


def side_by_side(table_ref, first, count):
    return jnp.concatenate([table_ref[first + i] for i in range(count)], 1)


def outer_forward(read_group, table_ref, planes_ref):
    start = 2 * (BLOCKS + 1)
    for group in range(INNER // GROUP):
        rows = pl.ds(group * GROUP, GROUP)
        block = read_group(rows).reshape(BLOCKS * GROUP, INNER)
        for half in range(2):
            wide = dot(side_by_side(table_ref, start + 2 * half, 2), block).astype(BF16)
            planes_ref[pl.ds(half * BLOCKS, BLOCKS), rows, :] = wide.reshape(BLOCKS, GROUP, INNER)


def inner_forward(freq, table_ref, planes_ref):
    if freq in (0, BLOCKS):
        both = dot(table_ref[freq], planes_ref[0 if freq == 0 else 1])
        return both[:INNER], -both[INNER:]
    both = dot(table_ref[freq], jnp.concatenate([planes_ref[2 * freq], planes_ref[2 * freq + 1]], 1))
    return both[:INNER, :INNER] + both[INNER:, INNER:], both[:INNER, INNER:] - both[INNER:, :INNER]


def inner_inverse(freq, re, im, table_ref, planes_ref):
    both = dot(table_ref[BLOCKS + 1 + freq], jnp.concatenate([re.astype(BF16), im.astype(BF16)], 1))
    back_re = (both[:INNER, :INNER] - both[INNER:, INNER:]).astype(BF16)
    if freq in (0, BLOCKS):
        planes_ref[0 if freq == 0 else 1] = back_re
    else:
        planes_ref[2 * freq] = back_re
        planes_ref[2 * freq + 1] = (both[INNER:, :INNER] + both[:INNER, INNER:]).astype(BF16)


def outer_inverse(group, table_ref, planes_ref):
    planes = planes_ref[:, pl.ds(group * GROUP, GROUP), :].reshape(2 * BLOCKS * GROUP, INNER)
    return dot(side_by_side(table_ref, 2 * (BLOCKS + 1) + 4, 4), planes).reshape(BLOCKS, GROUP, INNER)


def transform_table():
    outer, outer_back = outer_matrices()
    blocks = list(inner_matrices())
    for half in range(2):
        rows = outer[half * 2 * INNER : (half + 1) * 2 * INNER]
        blocks.append(np.stack([rows[:, :INNER], rows[:, INNER:]]))
    blocks.append(np.stack(np.split(outer_back, 4, axis=1)))
    return np.concatenate(blocks)


def convolve_kernel(pair_ref, table_ref, out_ref, spec_hbm, spec_ref, planes_ref, back_ref, semaphore):
    outer_forward(lambda rows: pair_ref[:, rows, :], table_ref, planes_ref)
    for freq in range(BLOCKS + 1):
        re, im = inner_forward(freq, table_ref, planes_ref)
        spec_ref[freq, :INNER] = re.astype(BF16)
        spec_ref[freq, INNER:] = im.astype(BF16)
        other_re, other_im = swap(re), swap(im)
        inner_inverse(freq, re * other_re - im * other_im, re * other_im + im * other_re, table_ref, back_ref)
    send = pltpu.make_async_copy(spec_ref, spec_hbm, semaphore)
    send.start()
    half_groups = INNER // GROUP // 2
    for group in range(half_groups):
        one = outer_inverse(group, table_ref, back_ref)
        two = outer_inverse(group + half_groups, table_ref, back_ref)
        packed = jnp.where(lane_low(one.shape), one, two)
        out_ref[:, pl.ds(group * GROUP, GROUP), :] = packed.astype(BF16)
    send.wait()


def correlate_kernel(grad_ref, spec_hbm, table_ref, out_ref, spec_ref, wide_ref, planes_ref, back_ref, semaphore):
    load = pltpu.make_async_copy(spec_hbm, spec_ref, semaphore)
    load.start()
    for block in range(BLOCKS):
        packed = grad_ref[block].astype(F32)
        turned = swap(packed)
        low = lane_low(packed.shape)
        wide_ref[block, :HALF] = jnp.where(low, packed, turned).astype(BF16)
        wide_ref[block, HALF:] = jnp.where(low, turned, packed).astype(BF16)
    outer_forward(lambda rows: wide_ref[:, rows, :], table_ref, planes_ref)
    load.wait()
    for freq in range(BLOCKS + 1):
        grad_re, grad_im = inner_forward(freq, table_ref, planes_ref)
        re, im = spec_ref[freq, :INNER].astype(F32), spec_ref[freq, INNER:].astype(F32)
        inner_inverse(freq, re * grad_re + im * grad_im, re * grad_im - im * grad_re, table_ref, back_ref)
    for group in range(INNER // GROUP):
        out_ref[:, pl.ds(group * GROUP, GROUP), :] = outer_inverse(group, table_ref, back_ref).astype(BF16)


def fetch(pairs, semaphores):
    copies = [pltpu.make_async_copy(source, target, semaphores.at[i]) for i, (source, target) in enumerate(pairs)]
    for copy in copies:
        copy.start()
    return copies


def gate_kernel(recv_ref, gate_ref, pre_ref, gated_ref, gate_grad_ref):
    for pair in range(BLOCKS // 2):
        conv = unfold_rows(recv_ref[2 * pair].astype(F32), recv_ref[2 * pair + 1].astype(F32))
        lanes = pl.ds(pair * INNER, INNER)
        gated_ref[:, lanes] = (gate_ref[:, lanes].astype(F32) * conv).astype(BF16)
        gate_grad_ref[:, lanes] = (pre_ref[:, lanes] * conv).astype(BF16)


def finish_kernel(scale, recv_ref, value_grad_ref, filter_grad_ref):
    for pair in range(BLOCKS // 2):
        first = recv_ref[2 * pair].astype(F32)
        second = recv_ref[2 * pair + 1].astype(F32)
        low = lane_low(first.shape)
        lanes = pl.ds(pair * INNER, INNER)
        filter_grad_ref[:, lanes] = jnp.where(low, first, swap(second)) * scale
        value_grad_ref[:, lanes] = jnp.where(low, swap(first), second).astype(BF16)


def stream_weight(weight_hbm, block_column, buffers, semaphores, count, use):
    depth, _, width = buffers.shape

    def copy(step):
        columns = pl.ds(pl.multiple_of(block_column(step) * width, width), width)
        return pltpu.make_async_copy(weight_hbm.at[:, columns], buffers.at[step % depth], semaphores.at[step % depth])

    for step in range(depth - 1):
        copy(step).start()
    for step in range(count):
        if step + depth - 1 < count:
            copy(step + depth - 1).start()
        copy(step).wait()
        use(step, buffers.at[step % depth])


DIRECT = 1


def column_rows(piece):
    if piece < DIRECT:
        return HALF + piece * INNER, INNER
    return HALF + DIRECT * INNER + (piece - DIRECT) * HALF, HALF


def gathered_block(spot_ref, step):
    depth, side = spot_ref[0], spot_ref[1]
    if step < 4:
        return 2 * step + side
    return 2 * lax.rem(depth + 8 - step, 4) + 1 - side


def pre_grad_kernel(spot_ref, near_ref, far0_ref, far1_ref, far2_ref, far3_ref, weight_hbm, gate_ref, *refs):
    total_ref, send_ref, buffers, semaphores = refs
    ring, rows, channels = near_ref.shape
    far = (far0_ref, far1_ref, far2_ref, far3_ref)
    upper = pl.ds(pl.multiple_of(lax.rem(spot_ref[0], 2) * HALF, HALF), HALF)

    def use(step, weight):
        block_ref = near_ref.at[step] if step < ring else far[step - ring]
        part = lax.dot_general(block_ref[...], weight[...], (((1,), (1,)), ((), ())), preferred_element_type=F32)
        total_ref[...] = part if step == 0 else total_ref[...] + part
        for half in range(2):
            target = 2 * gathered_block(spot_ref, step) + half
            start = half * (channels // 2)
            for piece in range(4):
                lanes = pl.ds(start + piece * INNER, INNER)
                place, size = column_rows(piece)
                send_ref[target, pl.ds(place, size)] = block_ref[:, lanes] if piece < DIRECT else block_ref[upper, lanes]

    stream_weight(weight_hbm, functools.partial(gathered_block, spot_ref), buffers, semaphores, 2 * ring, use)
    for pair in range(BLOCKS // 2):
        lanes = pl.ds(pair * INNER, INNER)
        first, second = fold_rows(total_ref[:, lanes] * gate_ref[:, lanes].astype(F32))
        send_ref[2 * pair, :HALF] = first.astype(BF16)
        send_ref[2 * pair + 1, :HALF] = second.astype(BF16)


def project_kernel(order, spot_ref, gated_ref, weight_hbm, *refs):
    out_refs, (buffers, semaphores) = refs[: len(order)], refs[len(order) :]
    depth, side = spot_ref[0], spot_ref[1]

    def column(step):
        layer = lax.rem(depth + order[step // 2], len(order))
        return 2 * layer + (side if step % 2 == 0 else 1 - side)

    def use(step, weight):
        out_refs[step // 2][step % 2] = dot(gated_ref[...], weight[...]).astype(BF16)

    stream_weight(weight_hbm, column, buffers, semaphores, 2 * len(order), use)


def weight_grad_kernel(scale, spot_ref, gated_hbm, received_hbm, shared_hbm, out_ref, gated_ref, wide_ref, total_ref, arrived, semaphores):
    parts = gated_ref.shape[0]
    side = lax.rem(spot_ref[0], 2)
    own = pl.ds(pl.multiple_of(side * HALF, HALF), HALF)
    other = pl.ds(pl.multiple_of((1 - side) * HALF, HALF), HALF)
    moves = []
    for piece in range(4):
        lanes = pl.ds(piece * INNER, INNER)
        place, size = column_rows(piece)
        source = received_hbm.at[:, pl.ds(place, size)]
        if piece < DIRECT:
            moves.append((source, wide_ref.at[:, :, lanes]))
        else:
            moves.append((source, wide_ref.at[:, own, lanes]))
            part = pl.ds((piece - DIRECT) * HALF, HALF)
            moves.append((shared_hbm.at[:, part], wide_ref.at[:, other, lanes]))
    copies = fetch(moves, semaphores)
    loads = fetch([(gated_hbm.at[part], gated_ref.at[part]) for part in range(parts)], arrived)
    for copy in copies:
        copy.wait()
    count, rows, width = wide_ref.shape
    tile = out_ref.shape[0] // 4
    for part in range(parts):
        loads[part].wait()
        columns = wide_ref[part * count // parts : (part + 1) * count // parts].reshape(-1, width)
        for first in range(0, out_ref.shape[0], tile):
            place = pl.ds(first, tile)
            total = lax.dot_general(
                gated_ref[part, :, place], columns, (((0,), (0,)), ((), ())), preferred_element_type=F32
            )
            if part > 0:
                total += total_ref[place]
            if part < parts - 1:
                total_ref[place] = total
            else:
                out_ref[place] = (total * scale).astype(BF16)


def add_kernel(kept_ref, other_ref, out_ref):
    out_ref[...] = (kept_ref[...] + other_ref[...].astype(F32)).astype(BF16)


def shape(dims, kind):
    return jax.ShapeDtypeStruct(dims, kind)


def params(mebibytes=16):
    return pltpu.CompilerParams(vmem_limit_bytes=mebibytes * 1024 * 1024)


def after(array, other):
    return lax.optimization_barrier((array, other))[0]


def exchange(array, axis, groups=None):
    return lax.all_to_all(array, axis, split_axis=0, concat_axis=0, tiled=True, axis_index_groups=groups)


def cost(microseconds):
    return pl.CostEstimate(flops=0, bytes_accessed=int(microseconds * 3.5e6), transcendentals=0)


def body(gate_input, value_input, filter_taps, out_weight, grad_output):
    rows, channels = gate_input.shape
    shards = lax.axis_size("seq")
    groups = lax.axis_size("ch")
    scale = 1.0 / math.sqrt(rows * shards)
    width = channels * groups // shards
    table = jnp.asarray(transform_table(), BF16)
    planes = pltpu.VMEM((2 * BLOCKS, INNER, INNER), BF16)
    spectra = pltpu.VMEM((BLOCKS + 1, 2 * INNER, INNER), BF16)
    anywhere = pl.BlockSpec(memory_space=pl.ANY)
    vmem = pl.BlockSpec(memory_space=pltpu.VMEM)
    smem = pl.BlockSpec(memory_space=pltpu.SMEM)
    place = lax.axis_index("ch")
    ring = groups // 2
    spot = jnp.stack([place // 2, place % 2]).astype(jnp.int32)
    ahead_by = lambda ahead: [(i, (i + 2 * ahead) % groups) for i in range(groups)]
    across = [(i, i ^ 1) for i in range(groups)]
    layers = [[2 * i + j for i in range(ring)] for j in range(2)]

    partner = lax.ppermute(grad_output, "ch", across)
    pair = pl.pallas_call(
        pack_kernel,
        out_shape=shape((shards, rows, INNER), BF16),
        compiler_params=params(60),
        cost_estimate=cost(2),
        name="pack",
    )(value_input, filter_taps)
    near = lax.all_gather(grad_output, "ch", axis=0, tiled=False, axis_index_groups=layers)
    far = [after(partner, pair)]
    far += [lax.ppermute(far[0], "ch", ahead_by(ahead)) for ahead in (1, 2, 3)]
    pair = exchange(after(pair, partner), "seq")
    packed, spec = pl.pallas_call(
        convolve_kernel,
        out_specs=(vmem, anywhere),
        out_shape=(shape((shards, HALF, INNER), BF16), shape((BLOCKS + 1, 2 * INNER, INNER), BF16)),
        scratch_shapes=[spectra, planes, planes, pltpu.SemaphoreType.DMA],
        compiler_params=params(16),
        cost_estimate=cost(3),
        name="convolve",
    )(pair, table)
    stream_scratch = [pltpu.VMEM((4, channels, channels), BF16), pltpu.SemaphoreType.DMA((4,))]
    direct = HALF + DIRECT * INNER
    depth = direct + (4 - DIRECT) * HALF
    pre_grad, send = pl.pallas_call(
        pre_grad_kernel,
        in_specs=[smem] + [vmem] * 5 + [anywhere, vmem],
        out_shape=(shape((rows, channels), F32), shape((shards, depth, INNER), BF16)),
        scratch_shapes=stream_scratch,
        compiler_params=params(50),
        cost_estimate=cost(9),
        name="pre_grad",
    )(spot, near, *far, out_weight, gate_input)
    gated, gate_grad = pl.pallas_call(
        gate_kernel,
        out_shape=[shape((rows, channels), BF16)] * 2,
        compiler_params=params(),
        cost_estimate=cost(1),
        name="gate",
    )(exchange(packed, "seq"), gate_input, pre_grad)

    gated_all = lax.all_gather(gated, "seq", axis=0, tiled=True)
    received = exchange(send, "seq")

    order = (2, 1, 3, 0)
    parts = pl.pallas_call(
        functools.partial(project_kernel, order),
        in_specs=[smem, vmem, anywhere],
        out_shape=[shape((2, rows, channels), BF16)] * ring,
        scratch_shapes=stream_scratch,
        compiler_params=params(50),
        cost_estimate=cost(8),
        name="project",
    )(spot, gated, out_weight)
    parts = [lax.ppermute(part, "ch", ahead_by(ahead)) if ahead else part for part, ahead in zip(parts, order)]

    part = received[:, direct:]
    shared = lax.ppermute(part, "ch", [(i, i ^ 2) for i in range(groups)])
    returned = pl.pallas_call(
        correlate_kernel,
        grid=(1,),
        out_shape=shape((shards, rows, INNER), BF16),
        in_specs=[pl.BlockSpec((shards, HALF, INNER), lambda step: (0, 0, 0)), anywhere, vmem],
        out_specs=vmem,
        scratch_shapes=[spectra, pltpu.VMEM((shards, rows, INNER), BF16), planes, planes, pltpu.SemaphoreType.DMA],
        compiler_params=params(16),
        cost_estimate=cost(3),
        name="correlate",
    )(after(received, part), spec, table)

    parts = [after(got, returned) for got in parts]
    opposite = sum(part[1].astype(F32) for part in parts).astype(BF16)
    kept = sum(part[0].astype(F32) for part in parts)
    returned = exchange(returned, "seq")

    opposite = lax.ppermute(opposite, "ch", across)

    weight_grad = pl.pallas_call(
        functools.partial(weight_grad_kernel, scale),
        in_specs=[smem, anywhere, anywhere, anywhere],
        out_shape=shape((channels, width), BF16),
        scratch_shapes=[
            pltpu.VMEM((4, shards * rows // 4, channels), BF16),
            pltpu.VMEM((shards, rows, width), BF16),
            pltpu.VMEM((channels, width), F32),
            pltpu.SemaphoreType.DMA((4,)),
            pltpu.SemaphoreType.DMA((8 - DIRECT,)),
        ],
        compiler_params=params(60),
        cost_estimate=cost(6),
        name="weight_grad",
    )(spot, gated_all.reshape(4, shards * rows // 4, channels), received, shared)
    value_grad, filter_grad = pl.pallas_call(
        functools.partial(finish_kernel, scale),
        out_shape=(shape((rows, channels), BF16), shape((rows, channels), F32)),
        compiler_params=params(),
        cost_estimate=cost(1),
        name="finish",
    )(after(returned, weight_grad))
    opposite = after(opposite, (weight_grad, value_grad))
    block_output = pl.pallas_call(
        add_kernel,
        out_shape=shape((rows, channels), BF16),
        compiler_params=params(),
        cost_estimate=cost(1),
        name="add_opposite",
    )(kept, opposite)
    return (block_output, gate_grad, value_grad, filter_grad, weight_grad)


def solution(mesh):
    placed = (P("seq", "ch"), P("seq", "ch"), P("seq", "ch"), P("ch", None), P("seq", "ch"))
    return jax.shard_map(
        body,
        mesh=mesh,
        in_specs=placed,
        out_specs=(P("seq", "ch"), P("seq", "ch"), P("seq", "ch"), P("seq", "ch"), P("ch", "seq")),
        check_vma=False,
    )
```
